256 devices in a mesh: grp: 8 (over x, core), ctx: 32 (over z, y).
Axes of the slice: x: 4, y: 4, z: 8, core: 2. Of those that a mesh axis runs over, the one named last changes fastest.
Arguments:
- queries: bfloat16 [32768, 8192], P(('grp', 'ctx')), may hold values from -160 to 160
- key_tensor: bfloat16 [32768, 512], P(('grp', 'ctx')), may hold values from -5 to 5
- value_tensor: bfloat16 [32768, 512], P(('grp', 'ctx')), may hold values from -6 to 6
- out_grad: bfloat16 [32768, 8192], P(('grp', 'ctx')), may hold values from -6 to 6
- doc_lengths: int32 [682], replicated, may hold values from 1 to 192, 32768 in all
- placement: int32 [64], replicated, may hold values from 0 to 63, each once
Outputs:
- attended: bfloat16 [32768, 8192], P(('grp', 'ctx'))
- query_grad: bfloat16 [32768, 8192], P(('grp', 'ctx'))
- key_grad: bfloat16 [32768, 512], P(('grp', 'ctx'))
- value_grad: bfloat16 [32768, 512], P(('grp', 'ctx'))
The draws below stay inside these ranges and needn't reach their ends.
Inputs may be any that keep to these rules, and one draw needn't show every extreme that they name: `doc_lengths`: the documents fill the window; one of them has exactly 192 tokens. `placement`: each block number appears once.
All inputs are finite; a program needn't handle non-finite values.
Results may differ from the reference program's by a relative error of at most 0.013.
Values may be sent and summed in bfloat16 or wider, within the bound.
No kernel may reach another device: no remote copies, remote signals or barrier semaphores. Data moves between devices by JAX's collectives and lax.ppermute only.
A program may use at most 128 MiB of HBM per device.

```python
import math
import jax
import jax.numpy as jnp
import numpy as np
from jax import lax

QUERY_HEADS = 64
KEY_VALUE_HEADS = 4
HEAD_SIZE = 128
TOK_DEV = 128
DOCUMENT_LIMIT = 192
SLOTS = 64
WINDOW_TOKENS = 32768
DOCS = 682
N_CTX = 32


def shared_keys(key):
    return jnp.clip(jax.random.normal(key, (WINDOW_TOKENS, KEY_VALUE_HEADS * HEAD_SIZE), jnp.float32), -5.0, 5.0)


def draw_key_tensor(key, part):
    base_offset = shared_keys(key)
    return base_offset.astype(jnp.bfloat16)


def draw_queries(key, part):
    key = jax.random.fold_in(key, 23)
    first_key = jax.random.fold_in(key, 0)
    noise = jax.random.normal(first_key, (WINDOW_TOKENS, QUERY_HEADS * HEAD_SIZE), jnp.float32)
    values_out = jnp.clip(noise, -6.0, 6.0)
    return values_out.astype(jnp.bfloat16)


def level_of(own_key, extent, cuts, smallest, high):
    gain = 1.0
    for dim, parts in cuts:
        steps = jax.random.uniform(jax.random.fold_in(jax.random.fold_in(own_key, 6), dim), (parts,), jnp.float32, smallest / len(cuts), high / len(cuts))
        gain = gain * jnp.repeat(jnp.exp(steps), extent[dim] // parts).reshape((-1,) + (1,) * (len(extent) - 1 - dim))
    return gain


def profile(amount, total, reach, lean):
    weights = [(1 << 20) // math.isqrt(rank ** lean) + 1 for rank in range(2, amount + 1)]
    spare, counts = total - reach - (amount - 1), [1] * (amount - 1)
    while spare > 0:
        free = [i for i in range(amount - 1) if counts[i] < reach]
        whole, budget = sum([weights[i] for i in free]), spare
        for i in free:
            addition = min(reach - counts[i], max(1, budget * weights[i] // whole), spare)
            counts[i] = counts[i] + addition
            spare = spare - addition
    return np.array([reach] + counts)


def uneven(own_key, amount, total, bound, skew):
    if amount == 2:
        one = jax.random.randint(own_key, (), max(1, total - bound), min(bound, total - 1) + 1)
        return jnp.stack([one, total - one])
    tallies = jnp.asarray(profile(amount, total, bound, skew), jnp.int32)
    couples = (amount - 1) // 2
    source_of, sink = tallies[1:1 + 2 * couples:2], tallies[2:2 + 2 * couples:2]
    slack = jnp.minimum(source_of - 1, bound - sink)
    passed = jax.random.randint(jax.random.fold_in(own_key, 1), (couples,), 0, 1 << 20) % (slack + 1)
    tallies = tallies.at[1:1 + 2 * couples:2].set(source_of - passed).at[2:2 + 2 * couples:2].set(sink + passed)
    return tallies[jax.random.permutation(jax.random.fold_in(own_key, 2), amount)]


def centred(rng, extent, scale, bound, cuts=(), kind=jnp.bfloat16):
    entries = scale * jax.random.normal(rng, extent, jnp.float32)
    if cuts:
        entries = entries * level_of(rng, extent, cuts, -0.22, 0.18)
    return jnp.clip(entries, -bound, bound).astype(kind)


def setup_inputs(seed: int = 0) -> dict:
    arg_keys = jax.random.split(jax.random.key(seed), 7)
    return {
        "queries": draw_queries(jax.random.fold_in(arg_keys[6], 71), 0),
        "key_tensor": draw_key_tensor(jax.random.fold_in(arg_keys[6], 71), 0),
        "value_tensor": centred(arg_keys[2], (WINDOW_TOKENS, KEY_VALUE_HEADS * HEAD_SIZE), 1.0, 6.0, ((0, 256),)),
        "out_grad": centred(arg_keys[3], (WINDOW_TOKENS, QUERY_HEADS * HEAD_SIZE), 1.0, 6.0, ((0, 256),)),
        "doc_lengths": uneven(arg_keys[4], DOCS, WINDOW_TOKENS, DOCUMENT_LIMIT, 2).astype(jnp.int32),
        "placement": jax.random.permutation(arg_keys[5], SLOTS).astype(jnp.int32),
    }


def document_start(positions, doc_starts):
    return lax.optimization_barrier(jnp.max(jnp.where(doc_starts[None, :] <= positions[:, None], doc_starts[None, :], 0), axis=1))

def attend(query_rows, key_rows, value_rows, gradient_rows, q_pos, k_pos, first_pos):
    row_total = query_rows.shape[0]
    span_length = key_rows.shape[0]
    group_width = QUERY_HEADS // KEY_VALUE_HEADS
    score_scale = 1.0 / math.sqrt(HEAD_SIZE)
    high = lax.Precision.HIGHEST
    query_piece = query_rows.reshape(row_total, KEY_VALUE_HEADS, group_width, HEAD_SIZE).astype(jnp.float32)
    key_piece = key_rows.reshape(span_length, KEY_VALUE_HEADS, HEAD_SIZE).astype(jnp.float32)
    value_piece = value_rows.reshape(span_length, KEY_VALUE_HEADS, HEAD_SIZE).astype(jnp.float32)
    gradient_piece = gradient_rows.reshape(row_total, KEY_VALUE_HEADS, group_width, HEAD_SIZE).astype(jnp.float32)
    scores = jnp.einsum('qhgd,whd->hgqw', query_piece, key_piece, precision=high) * score_scale
    allowed = (k_pos[None, :] <= q_pos[:, None]) & (k_pos[None, :] >= first_pos[:, None])
    scores = jnp.where(allowed, scores, -1e+30)
    row_top = lax.optimization_barrier(jnp.max(scores, axis=-1, keepdims=True))
    weights_raw = jnp.where(allowed, jnp.exp(scores - row_top), 0.0)
    weights = weights_raw / lax.optimization_barrier(jnp.sum(weights_raw, axis=-1, keepdims=True))
    weights_low = lax.optimization_barrier(weights.astype(jnp.bfloat16)).astype(jnp.float32)
    output = jnp.einsum('hgqw,whd->qhgd', weights_low, value_piece, precision=high)
    output_lowered = lax.optimization_barrier(output.astype(jnp.bfloat16))
    row_delta = lax.optimization_barrier(jnp.sum(gradient_piece * output_lowered.astype(jnp.float32), axis=-1))
    dprob = jnp.einsum('qhgd,whd->hgqw', gradient_piece, value_piece, precision=high)
    dscore = weights * (dprob - jnp.transpose(row_delta, (1, 2, 0))[..., None]) * score_scale
    dscore = lax.optimization_barrier(dscore.astype(jnp.bfloat16)).astype(jnp.float32)
    query_gradient = jnp.einsum('hgqw,whd->qhgd', dscore, key_piece, precision=high)
    key_gradient = jnp.einsum('hgqw,qhgd->whd', dscore, query_piece, precision=high)
    value_gradient = jnp.einsum('hgqw,qhgd->whd', weights_low, gradient_piece, precision=high)
    return (output_lowered.reshape(row_total, QUERY_HEADS * HEAD_SIZE), query_gradient.astype(jnp.bfloat16).reshape(row_total, QUERY_HEADS * HEAD_SIZE), key_gradient.reshape(span_length, KEY_VALUE_HEADS * HEAD_SIZE), value_gradient.reshape(span_length, KEY_VALUE_HEADS * HEAD_SIZE))

def reference(queries, key_tensor, value_tensor, out_grad, doc_lengths, placement):
    group_tokens = TOK_DEV * N_CTX
    block_len = TOK_DEV // 2
    row_ids = jnp.arange(WINDOW_TOKENS, dtype=jnp.int32)
    slot_ids = row_ids % group_tokens // block_len
    positions = (row_ids // group_tokens * group_tokens + placement[slot_ids] * block_len + row_ids % block_len).astype(jnp.int32)
    row_at = jnp.zeros((WINDOW_TOKENS,), jnp.int32).at[positions].set(row_ids)
    doc_ends = jnp.cumsum(doc_lengths).astype(jnp.int32)
    doc_starts = (doc_ends - doc_lengths).astype(jnp.int32)
    blocks = (WINDOW_TOKENS + DOCUMENT_LIMIT - 1) // DOCUMENT_LIMIT
    padding_count = blocks * DOCUMENT_LIMIT - WINDOW_TOKENS
    tail_q = jnp.zeros((padding_count, QUERY_HEADS * HEAD_SIZE), queries.dtype)
    tail_key_value = jnp.zeros((padding_count, KEY_VALUE_HEADS * HEAD_SIZE), key_tensor.dtype)
    q_sorted = jnp.concatenate([queries[row_at], tail_q], axis=0)
    g_sorted = jnp.concatenate([out_grad[row_at], tail_q], axis=0)
    front_part = jnp.zeros((DOCUMENT_LIMIT, KEY_VALUE_HEADS * HEAD_SIZE), key_tensor.dtype)
    k_padded = jnp.concatenate([front_part, key_tensor[row_at], tail_key_value], axis=0)
    v_padded = jnp.concatenate([front_part, value_tensor[row_at], tail_key_value], axis=0)

    def one_block(index):
        first = index * DOCUMENT_LIMIT
        q_pos = (first + jnp.arange(DOCUMENT_LIMIT, dtype=jnp.int32)).astype(jnp.int32)
        k_pos = (first - DOCUMENT_LIMIT + jnp.arange(2 * DOCUMENT_LIMIT, dtype=jnp.int32)).astype(jnp.int32)
        return attend(lax.dynamic_slice_in_dim(q_sorted, first, DOCUMENT_LIMIT, 0), lax.dynamic_slice_in_dim(k_padded, first, 2 * DOCUMENT_LIMIT, 0), lax.dynamic_slice_in_dim(v_padded, first, 2 * DOCUMENT_LIMIT, 0), lax.dynamic_slice_in_dim(g_sorted, first, DOCUMENT_LIMIT, 0), q_pos, k_pos, document_start(q_pos, doc_starts))
    attended, query_grad, key_piece, value_piece = lax.map(one_block, jnp.arange(blocks, dtype=jnp.int32))

    def spread(part):
        total = jnp.zeros((blocks + 1, DOCUMENT_LIMIT, part.shape[-1]), jnp.float32)
        total = total.at[:blocks].add(part[:, :DOCUMENT_LIMIT]).at[1:].add(part[:, DOCUMENT_LIMIT:])
        return total[1:].reshape(blocks * DOCUMENT_LIMIT, part.shape[-1])[:WINDOW_TOKENS][positions].astype(jnp.bfloat16)
    return (attended.reshape(blocks * DOCUMENT_LIMIT, QUERY_HEADS * HEAD_SIZE)[:WINDOW_TOKENS][positions], query_grad.reshape(blocks * DOCUMENT_LIMIT, QUERY_HEADS * HEAD_SIZE)[:WINDOW_TOKENS][positions], spread(key_piece), spread(value_piece))
```

```python
import functools
import math

import jax
import jax.numpy as jnp
from jax import lax
from jax.experimental import pallas as pl
from jax.experimental.pallas import tpu as pltpu
from jax.sharding import PartitionSpec as P

KV_HEADS = 4
GROUP_WIDTH = 16
HEAD = 128
LIMIT = 192
BLOCK = 64
SLOTS = 64
BEFORE = LIMIT // BLOCK
ROWS = 16
PARTS = BLOCK // ROWS
PIECES = 2 * KV_HEADS * PARTS
CHUNK = 4
SCALE = 1.0 / math.sqrt(HEAD)
LOG2E = math.log2(math.e)

VMEM = pl.BlockSpec(memory_space=pltpu.VMEM)
SMEM = pl.BlockSpec(memory_space=pltpu.SMEM)


def pack_kernel(k_ref, v_ref, out_ref):
    for tensor, ref in enumerate((k_ref, v_ref)):
        for head in range(KV_HEADS):
            for part in range(PARTS):
                piece = (tensor * KV_HEADS + head) * PARTS + part
                for half in range(2):
                    out_ref[piece, half] = ref[
                        pl.ds(half * BLOCK + part * ROWS, ROWS), pl.ds(head * HEAD, HEAD)
                    ]


def last_kernel(place_ref, pieces_ref, out_ref):
    def one(slot, carry):
        block = place_ref[slot]

        @pl.when(block >= SLOTS - BEFORE)
        def _():
            out_ref[block - (SLOTS - BEFORE)] = pieces_ref[slot]

        return carry

    lax.fori_loop(0, SLOTS, one, 0)


def spread_kernel(place_ref, pieces_ref, prev_ref, out_ref, ordered):
    ordered[:BEFORE] = prev_ref[...]

    def put(slot, carry):
        ordered[place_ref[slot] + BEFORE] = pieces_ref[slot]
        return carry

    lax.fori_loop(0, SLOTS, put, 0, unroll=8)

    def take(slot, carry):
        block = place_ref[slot]
        for back in range(BEFORE):
            out_ref[slot, back] = ordered[block + back]
        return carry

    lax.fori_loop(0, SLOTS, take, 0, unroll=8)


def head_kernel(place_ref, parts_ref, out_ref, total):
    total[...] = jnp.zeros_like(total)

    def one(slot, carry):
        block = place_ref[slot]

        @pl.when(block < BEFORE)
        def _():
            for back in range(BEFORE):
                total[block + back] += parts_ref[slot, back].astype(jnp.float32)

        return carry

    lax.fori_loop(0, SLOTS, one, 0)
    out_ref[...] = total[:BEFORE].astype(jnp.bfloat16)


def sum_kernel(place_ref, parts_ref, next_ref, out_ref, total):
    total[...] = jnp.zeros_like(total)
    total[SLOTS:] = next_ref[...].astype(jnp.float32)

    def add(slot, carry):
        block = place_ref[slot]
        for back in range(BEFORE):
            total[block + back] += parts_ref[slot, back].astype(jnp.float32)
        return carry

    lax.fori_loop(0, SLOTS, add, 0, unroll=4)

    def take(slot, carry):
        out_ref[slot] = total[place_ref[slot] + BEFORE].astype(jnp.bfloat16)
        return carry

    lax.fori_loop(0, SLOTS, take, 0, unroll=8)


def finish_kernel(pieces_ref, dk_ref, dv_ref, out_k_ref, out_v_ref):
    for tensor, (own, out) in enumerate(((dk_ref, out_k_ref), (dv_ref, out_v_ref))):
        for head in range(KV_HEADS):
            for part in range(PARTS):
                piece = (tensor * KV_HEADS + head) * PARTS + part
                for half in range(2):
                    place = (
                        pl.ds(half * BLOCK + part * ROWS, ROWS),
                        pl.ds(head * HEAD, HEAD),
                    )
                    out[place] = (
                        own[place] + pieces_ref[piece, half].astype(jnp.float32)
                    ).astype(jnp.bfloat16)


def attend_kernel(
    low_ref, q_ref, g_ref, k_ref, v_ref, far_ref,
    att_ref, dq_ref, far_grad_ref, dk_ref, dv_ref, bias_ref,
):
    half = pl.program_id(0)
    head = pl.program_id(1)
    span = LIMIT + BLOCK
    lanes = CHUNK * BLOCK

    @pl.when(head == 0)
    def _():
        key_index = lax.broadcasted_iota(jnp.int32, (span, lanes), 0)
        query_index = lax.broadcasted_iota(jnp.int32, (span, lanes), 1) % BLOCK
        allowed = (key_index <= query_index + LIMIT) & (key_index >= low_ref[0])
        bias_ref[...] = jnp.where(allowed, 0.0, -1e30)

    def keys_of(tensor, own_ref):
        far = [
            far_ref[tensor, head, part, half, back]
            for back in range(BEFORE)
            for part in range(PARTS)
        ]
        return jnp.concatenate(far + [own_ref[...]], axis=0)

    keys = keys_of(0, k_ref)
    values = keys_of(1, v_ref)
    keys_t = keys.T
    values_t = values.T

    def rows_of(ref, first):
        return jnp.concatenate(
            [ref[:, pl.ds((first + i) * HEAD, HEAD)] for i in range(CHUNK)], axis=0
        )

    def put(ref, first, cols):
        rows = cols.T.astype(jnp.bfloat16)
        for i in range(CHUNK):
            ref[:, pl.ds((first + i) * HEAD, HEAD)] = rows[i * BLOCK : (i + 1) * BLOCK]

    nt = (((1,), (1,)), ((), ()))
    nn = (((1,), (0,)), ((), ()))
    dot = functools.partial(lax.dot_general, preferred_element_type=jnp.float32)
    key_grad = jnp.zeros((span, HEAD), jnp.float32)
    value_grad = jnp.zeros((span, HEAD), jnp.float32)
    for first in range(0, GROUP_WIDTH, CHUNK):
        query = rows_of(q_ref, first)
        grad = rows_of(g_ref, first)
        scores = dot(keys, query, nt) * (SCALE * LOG2E) + bias_ref[...]
        dprob = dot(values, grad, nt)
        raw = jnp.exp2(scores - jnp.max(scores, axis=0, keepdims=True))
        weights = raw * (1.0 / jnp.sum(raw, axis=0, keepdims=True))
        weights_low = weights.astype(jnp.bfloat16)
        out_t = dot(values_t, weights_low, nn)
        put(att_ref, first, out_t)
        delta = jnp.sum(weights * dprob, axis=0, keepdims=True)
        dscore = (weights * (dprob - delta)).astype(jnp.bfloat16)
        put(dq_ref, first, dot(keys_t, dscore, nn) * SCALE)
        key_grad += dot(dscore, query, nn)
        value_grad += dot(weights_low, grad, nn)
    key_grad *= SCALE
    for tensor, grads, own in ((0, key_grad, dk_ref), (1, value_grad, dv_ref)):
        low = grads[:LIMIT].astype(jnp.bfloat16)
        for back in range(BEFORE):
            for part in range(PARTS):
                row = back * BLOCK + part * ROWS
                far_grad_ref[tensor, head, part, half, back] = low[row : row + ROWS]
        own[...] = grads[LIMIT:]


def attend(low, queries, key_tensor, value_tensor, out_grad, far):
    span = LIMIT + BLOCK
    wide = pl.BlockSpec((BLOCK, GROUP_WIDTH * HEAD), lambda j, h: (j, h))
    narrow = pl.BlockSpec((BLOCK, HEAD), lambda j, h: (j, h))
    return pl.pallas_call(
        attend_kernel,
        grid=(2, KV_HEADS),
        in_specs=[
            pl.BlockSpec((1, 1, CHUNK * BLOCK), lambda j, h: (j, 0, 0)),
            wide, wide, narrow, narrow, VMEM,
        ],
        out_specs=[wide, wide, VMEM, narrow, narrow],
        out_shape=[
            jax.ShapeDtypeStruct(queries.shape, jnp.bfloat16),
            jax.ShapeDtypeStruct(queries.shape, jnp.bfloat16),
            jax.ShapeDtypeStruct(far.shape, jnp.bfloat16),
            jax.ShapeDtypeStruct(key_tensor.shape, jnp.float32),
            jax.ShapeDtypeStruct(value_tensor.shape, jnp.float32),
        ],
        scratch_shapes=[pltpu.VMEM((span, CHUNK * BLOCK), jnp.float32)],
        compiler_params=pltpu.CompilerParams(
            dimension_semantics=("arbitrary", "arbitrary"),
            vmem_limit_bytes=40 * 1024 * 1024,
        ),
    )(low, queries, out_grad, key_tensor, value_tensor, far)


def call(kernel, outs, specs, *args, scratch=()):
    return pl.pallas_call(
        kernel,
        in_specs=specs,
        out_specs=[VMEM] * len(outs),
        out_shape=outs,
        scratch_shapes=scratch,
        compiler_params=pltpu.CompilerParams(vmem_limit_bytes=16 * 1024 * 1024),
    )(*args)


def body(queries, key_tensor, value_tensor, out_grad, doc_lengths, placement):
    ctx_count = lax.axis_size("ctx")
    grp_count = lax.axis_size("grp")
    ctx_index = lax.axis_index("ctx")
    grp_index = lax.axis_index("grp")
    tile = (ROWS, HEAD)
    bf16 = functools.partial(jax.ShapeDtypeStruct, dtype=jnp.bfloat16)
    exchange = functools.partial(
        lax.all_to_all, axis_name="ctx", split_axis=0, concat_axis=0, tiled=True
    )

    (packed,) = call(
        pack_kernel, [bf16((PIECES, 2, *tile))], [VMEM, VMEM], key_tensor, value_tensor
    )
    pieces = exchange(packed).reshape(SLOTS, *tile)
    (last,) = call(last_kernel, [bf16((BEFORE, *tile))], [SMEM, VMEM], placement, pieces)
    prev = lax.ppermute(last, "grp", [(i, i + 1) for i in range(grp_count - 1)])
    (wanted,) = call(
        spread_kernel,
        [bf16((SLOTS, BEFORE, *tile))],
        [SMEM, VMEM, VMEM],
        placement,
        pieces,
        prev,
        scratch=[pltpu.VMEM((SLOTS + BEFORE, *tile), jnp.bfloat16)],
    )
    far = exchange(wanted.reshape(ctx_count, 2, BEFORE, *tile))

    doc_ends = jnp.cumsum(doc_lengths)
    doc_starts = doc_ends - doc_lengths
    blocks = lax.dynamic_slice_in_dim(placement, 2 * ctx_index, 2)
    start = (grp_index * SLOTS + blocks) * BLOCK
    q_pos = (start[:, None] + jnp.arange(BLOCK, dtype=jnp.int32)).reshape(-1)
    first = jnp.max(
        jnp.where(doc_starts[None, :] <= q_pos[:, None], doc_starts[None, :], 0), axis=1
    )
    low = first.reshape(2, BLOCK) - (start - LIMIT)[:, None]
    low = jnp.tile(low, (1, CHUNK)).reshape(2, 1, CHUNK * BLOCK)

    attended, query_grad, far_grad, own_k, own_v = attend(
        low, queries, key_tensor, value_tensor, out_grad,
        far.reshape(2, KV_HEADS, PARTS, 2, BEFORE, *tile),
    )

    parts = exchange(far_grad.reshape(ctx_count, 2, BEFORE, *tile))
    parts = parts.reshape(SLOTS, BEFORE, *tile)
    (ahead,) = call(
        head_kernel,
        [bf16((BEFORE, *tile))],
        [SMEM, VMEM],
        placement,
        parts,
        scratch=[pltpu.VMEM((2 * BEFORE, *tile), jnp.float32)],
    )
    behind = lax.ppermute(ahead, "grp", [(i + 1, i) for i in range(grp_count - 1)])
    (sums,) = call(
        sum_kernel,
        [bf16((SLOTS, *tile))],
        [SMEM, VMEM, VMEM],
        placement,
        parts,
        behind,
        scratch=[pltpu.VMEM((SLOTS + BEFORE, *tile), jnp.float32)],
    )
    sums = exchange(sums.reshape(ctx_count, 2, *tile))
    key_grad, value_grad = call(
        finish_kernel,
        [bf16(key_tensor.shape), bf16(value_tensor.shape)],
        [VMEM] * 3,
        sums,
        own_k,
        own_v,
    )
    return attended, query_grad, key_grad, value_grad


def solution(mesh):
    rows = P(("grp", "ctx"), None)
    return jax.shard_map(
        body,
        mesh=mesh,
        in_specs=(rows, rows, rows, rows, P(), P()),
        out_specs=(rows, rows, rows, rows),
        check_vma=False,
    )
```

```python
import functools
import math

import jax
import jax.numpy as jnp
from jax import lax
from jax.experimental import pallas as pl
from jax.experimental.pallas import tpu as pltpu
from jax.sharding import PartitionSpec as P

KV_HEADS = 4
GROUP_WIDTH = 16
HEAD = 128
LIMIT = 192
BLOCK = 64
SLOTS = 64
BEFORE = LIMIT // BLOCK
ROWS = 16
PARTS = BLOCK // ROWS
PIECES = 2 * KV_HEADS * PARTS
CHUNK = 4
SCALE = 1.0 / math.sqrt(HEAD)
LOG2E = math.log2(math.e)
MIB = 1024 * 1024

VMEM = pl.BlockSpec(memory_space=pltpu.VMEM)
SMEM = pl.BlockSpec(memory_space=pltpu.SMEM)
ANY = pl.BlockSpec(memory_space=pltpu.HBM)


def pack_kernel(rows_ref, out_ref):
    for tensor in range(2):
        for head in range(KV_HEADS):
            for part in range(PARTS):
                piece = (tensor * KV_HEADS + head) * PARTS + part
                for half in range(2):
                    out_ref[piece, half] = rows_ref[
                        tensor,
                        pl.ds(half * BLOCK + part * ROWS, ROWS),
                        pl.ds(head * HEAD, HEAD),
                    ]


def order_kernel(place_ref, pieces_ref, ordered_ref, last_ref):
    for slot in range(SLOTS):
        ordered_ref[place_ref[slot]] = pieces_ref[slot]
    last_ref[...] = ordered_ref[SLOTS - BEFORE :]


def spread_kernel(place_ref, ordered_ref, prev_ref, out_ref, done_ref, whole):
    whole[:BEFORE] = prev_ref[...]
    whole[BEFORE:] = ordered_ref[...]
    done_ref[...] = jnp.zeros_like(done_ref)
    for slot in range(SLOTS):
        out_ref[slot] = whole[pl.ds(place_ref[slot], BEFORE)]


def slots_of(place_ref, slot_of):
    for slot in range(SLOTS):
        slot_of[place_ref[slot]] = slot


def part_sum(slot_of, parts_ref, block):
    return sum(
        parts_ref[slot_of[block + ahead], BEFORE - ahead].astype(jnp.float32)
        for ahead in range(1, BEFORE + 1)
        if 0 <= block + ahead < SLOTS
    )


def head_kernel(place_ref, parts_ref, after_ref, out_ref, slot_of):
    slots_of(place_ref, slot_of)
    for back in range(BEFORE):
        out_ref[back] = part_sum(slot_of, parts_ref, back - BEFORE).astype(jnp.bfloat16)


def sum_kernel(place_ref, parts_ref, sums_ref, tail_ref, slot_of):
    slots_of(place_ref, slot_of)
    for block in range(SLOTS - 1):
        total = part_sum(slot_of, parts_ref, block)
        sums_ref[slot_of[block]] = total.astype(jnp.bfloat16)
        if block >= SLOTS - BEFORE:
            tail_ref[block - (SLOTS - BEFORE)] = total
    tail_ref[BEFORE - 1] = jnp.zeros((ROWS, HEAD), jnp.float32)


def tail_kernel(place_ref, sums_ref, tail_ref, next_ref, out_ref, slot_of):
    out_ref[...] = sums_ref[...]
    slots_of(place_ref, slot_of)
    for tail in range(BEFORE):
        total = tail_ref[tail] + next_ref[tail].astype(jnp.float32)
        out_ref[slot_of[SLOTS - BEFORE + tail]] = total.astype(jnp.bfloat16)


def finish_kernel(pieces_ref, dk_ref, dv_ref, out_k_ref, out_v_ref):
    for tensor, (own, out) in enumerate(((dk_ref, out_k_ref), (dv_ref, out_v_ref))):
        for head in range(KV_HEADS):
            for part in range(PARTS):
                piece = (tensor * KV_HEADS + head) * PARTS + part
                for half in range(2):
                    place = (
                        pl.ds(half * BLOCK + part * ROWS, ROWS),
                        pl.ds(head * HEAD, HEAD),
                    )
                    out[place] = (
                        own[place] + pieces_ref[piece, half].astype(jnp.float32)
                    ).astype(jnp.bfloat16)


def rows_of(ref, first, width=CHUNK):
    return jnp.concatenate(
        [ref[:, pl.ds((first + i) * HEAD, HEAD)] for i in range(width)], axis=0
    )


NT = (((1,), (1,)), ((), ()))
NN = (((1,), (0,)), ((), ()))
dot = functools.partial(lax.dot_general, preferred_element_type=jnp.float32)


def mask_to(bias_ref, low_ref, first_key):
    keys, lanes = bias_ref.shape
    key_index = first_key + lax.broadcasted_iota(jnp.int32, (keys, lanes), 0)
    query_index = lax.broadcasted_iota(jnp.int32, (keys, lanes), 1) % BLOCK
    allowed = (key_index <= query_index + LIMIT) & (key_index >= low_ref[0])
    bias_ref[...] = jnp.where(allowed, 0.0, -1e30)


def far_rows(far_ref, tensor, head, half):
    return [
        far_ref[tensor, head, part, half, back]
        for back in range(BEFORE)
        for part in range(PARTS)
    ]


def own_kernel(
    low_ref, q_ref, g_ref, k_ref, v_ref, after_ref, stat_ref, bias_ref
):
    key_index = LIMIT + lax.broadcasted_iota(jnp.int32, bias_ref.shape[1:], 0)
    query_index = lax.broadcasted_iota(jnp.int32, bias_ref.shape[1:], 1) % BLOCK
    for half in range(2):
        allowed = (key_index <= query_index + LIMIT) & (key_index >= low_ref[half])
        bias_ref[half] = jnp.where(allowed, 0.0, -1e30)

    for half in range(2):
        rows = pl.ds(half * BLOCK, BLOCK)
        for head in range(KV_HEADS):
            cols = pl.ds(head * HEAD, HEAD)
            for first in range(0, GROUP_WIDTH, CHUNK):
                lanes = pl.ds(first * BLOCK, CHUNK * BLOCK)
                query = rows_of(q_ref.at[rows], head * GROUP_WIDTH + first)
                grad = rows_of(g_ref.at[rows], head * GROUP_WIDTH + first)
                scores = dot(k_ref[rows, cols], query, NT) * (SCALE * LOG2E) + bias_ref[half]
                dprob = dot(v_ref[rows, cols], grad, NT)
                top = jnp.max(scores, axis=0, keepdims=True)
                raw = jnp.exp2(scores - top)
                stat_ref[half, head, 0:1, lanes] = top
                stat_ref[half, head, 1:2, lanes] = jnp.sum(raw, axis=0, keepdims=True)
                stat_ref[half, head, 2:3, lanes] = jnp.sum(raw * dprob, axis=0, keepdims=True)


def far_kernel(
    low_ref, q_ref, g_ref, stat_ref, far_ref, far_grad_ref, low_out_ref,
    bias_ref, q_rows, g_rows, sems,
):
    steps = [(half, head) for half in range(2) for head in range(KV_HEADS)]
    cuts = (0, 1, 4, 8)
    loads = {}
    for i, (first, last) in enumerate(zip(cuts[:-1], cuts[1:])):
        half, head = steps[first]
        place = (
            pl.ds(half * BLOCK, BLOCK),
            pl.ds(head * GROUP_WIDTH * HEAD, (last - first) * GROUP_WIDTH * HEAD),
        )
        loads[first] = [
            pltpu.make_async_copy(ref.at[place], rows.at[place], sems.at[i, j])
            for j, (ref, rows) in enumerate(((q_ref, q_rows), (g_ref, g_rows)))
        ]
        for load in loads[first]:
            load.start()
    low_out_ref[...] = low_ref[...]
    lanes = GROUP_WIDTH * BLOCK
    key_index = lax.broadcasted_iota(jnp.int32, (LIMIT, CHUNK * BLOCK), 0)
    for half in range(2):
        bias = jnp.where(key_index >= low_ref[half], 0.0, -1e30)
        bias_ref[half] = jnp.concatenate([bias] * (GROUP_WIDTH // CHUNK), axis=1)

    for step, (half, head) in enumerate(steps):
        rows = pl.ds(half * BLOCK, BLOCK)
        for load in loads.get(step, ()):
            load.wait()
        first = head * GROUP_WIDTH
        keys = jnp.concatenate(far_rows(far_ref, 0, head, half), axis=0)
        values = jnp.concatenate(far_rows(far_ref, 1, head, half), axis=0)
        query = rows_of(q_rows.at[rows], first, GROUP_WIDTH)
        grad = rows_of(g_rows.at[rows], first, GROUP_WIDTH)
        scores = dot(keys, query, NT) * (SCALE * LOG2E) + bias_ref[half]
        dprob = dot(values, grad, NT)
        own_top, own_total, own_delta = [
            stat_ref[half, head, i : i + 1, :lanes] for i in range(3)
        ]
        top = jnp.maximum(own_top, jnp.max(scores, axis=0, keepdims=True))
        raw = jnp.exp2(scores - top)
        fade = jnp.exp2(own_top - top)
        total = own_total * fade + jnp.sum(raw, axis=0, keepdims=True)
        delta = own_delta * fade + jnp.sum(raw * dprob, axis=0, keepdims=True)
        share = 1.0 / total
        weights = raw * share
        dscore = (weights * (dprob - delta * share)).astype(jnp.bfloat16)
        key_grad = dot(dscore, query, NN) * SCALE
        value_grad = dot(weights.astype(jnp.bfloat16), grad, NN)
        for tensor, grads in ((0, key_grad), (1, value_grad)):
            rounded = grads.astype(jnp.bfloat16)
            for back in range(BEFORE):
                for part in range(PARTS):
                    row = back * BLOCK + part * ROWS
                    far_grad_ref[tensor, head, part, half, back] = rounded[row : row + ROWS]


def rest_kernel(
    low_ref, q_ref, g_ref, k_ref, v_ref, far_ref, att_ref, dq_ref, dk_ref, dv_ref, bias_ref
):
    half = pl.program_id(0)
    head = pl.program_id(1)

    @pl.when(head == 0)
    def _():
        mask_to(bias_ref, low_ref, 0)

    keys = jnp.concatenate(far_rows(far_ref, 0, head, half) + [k_ref[...]], axis=0)
    values = jnp.concatenate(far_rows(far_ref, 1, head, half) + [v_ref[...]], axis=0)
    keys_t = keys.T
    values_t = values.T

    def put(ref, first, cols):
        rows = cols.T.astype(jnp.bfloat16)
        for i in range(CHUNK):
            ref[:, pl.ds((first + i) * HEAD, HEAD)] = rows[i * BLOCK : (i + 1) * BLOCK]

    key_grad = jnp.zeros((BLOCK, HEAD), jnp.float32)
    value_grad = jnp.zeros((BLOCK, HEAD), jnp.float32)
    for first in range(0, GROUP_WIDTH, CHUNK):
        query = rows_of(q_ref, first)
        grad = rows_of(g_ref, first)
        scores = dot(keys, query, NT) * (SCALE * LOG2E) + bias_ref[...]
        dprob = dot(values, grad, NT)
        raw = jnp.exp2(scores - jnp.max(scores, axis=0, keepdims=True))
        weights = raw * (1.0 / jnp.sum(raw, axis=0, keepdims=True))
        weights_low = weights.astype(jnp.bfloat16)
        put(att_ref, first, dot(values_t, weights_low, NN))
        delta = jnp.sum(weights * dprob, axis=0, keepdims=True)
        dscore = (weights * (dprob - delta)).astype(jnp.bfloat16)
        put(dq_ref, first, dot(keys_t, dscore, NN) * SCALE)
        key_grad += dot(dscore[LIMIT:], query, NN)
        value_grad += dot(weights_low[LIMIT:], grad, NN)
    dk_ref[...] = key_grad * SCALE
    dv_ref[...] = value_grad


LOW = pl.BlockSpec((1, 1, CHUNK * BLOCK), lambda j, h: (j, 0, 0))
WIDE = pl.BlockSpec((BLOCK, GROUP_WIDTH * HEAD), lambda j, h: (j, h))
NARROW = pl.BlockSpec((BLOCK, HEAD), lambda j, h: (j, h))
STAT = pl.BlockSpec((1, 1, 8, GROUP_WIDTH * BLOCK), lambda j, h: (j, h, 0, 0))


def grid_call(kernel, keys, in_specs, out_specs, out_shape, *args):
    return pl.pallas_call(
        kernel,
        grid=(2, KV_HEADS),
        in_specs=in_specs,
        out_specs=out_specs,
        out_shape=out_shape,
        scratch_shapes=[pltpu.VMEM((keys, CHUNK * BLOCK), jnp.float32)],
        compiler_params=pltpu.CompilerParams(
            dimension_semantics=("arbitrary", "arbitrary"),
            vmem_limit_bytes=24 * MIB,
        ),
    )(*args)


def attend_own(low, queries, out_grad, key_tensor, value_tensor, after):
    return call(
        own_kernel,
        [jax.ShapeDtypeStruct((2, KV_HEADS, 8, GROUP_WIDTH * BLOCK), jnp.float32)],
        [VMEM] * 5 + [ANY],
        low, queries, out_grad, key_tensor, value_tensor, after,
        scratch=[pltpu.VMEM((2, BLOCK, CHUNK * BLOCK), jnp.float32)],
        limit=24 * MIB,
    )


def attend_far(low, queries, out_grad, stat, far):
    return call(
        far_kernel,
        [
            jax.ShapeDtypeStruct(far.shape, jnp.bfloat16),
            jax.ShapeDtypeStruct(low.shape, jnp.int32),
        ],
        [VMEM, ANY, ANY, VMEM, VMEM],
        low, queries, out_grad, stat, far,
        scratch=[
            pltpu.VMEM((2, LIMIT, GROUP_WIDTH * BLOCK), jnp.float32),
            pltpu.VMEM(queries.shape, jnp.bfloat16),
            pltpu.VMEM(queries.shape, jnp.bfloat16),
            pltpu.SemaphoreType.DMA((3, 2)),
        ],
        limit=52 * MIB,
    )


def attend_rest(low, queries, out_grad, key_tensor, value_tensor, far):
    wide = jax.ShapeDtypeStruct(queries.shape, jnp.bfloat16)
    narrow = jax.ShapeDtypeStruct(key_tensor.shape, jnp.float32)
    return grid_call(
        rest_kernel, LIMIT + BLOCK, [LOW, WIDE, WIDE, NARROW, NARROW, VMEM],
        [WIDE, WIDE, NARROW, NARROW], [wide, wide, narrow, narrow],
        low, queries, out_grad, key_tensor, value_tensor, far,
    )


def call(kernel, outs, specs, *args, out_specs=None, scratch=(), limit=8 * MIB):
    return pl.pallas_call(
        kernel,
        in_specs=specs,
        out_specs=out_specs or [VMEM] * len(outs),
        out_shape=outs,
        scratch_shapes=scratch,
        compiler_params=pltpu.CompilerParams(vmem_limit_bytes=limit),
    )(*args)


def body(queries, key_tensor, value_tensor, out_grad, doc_lengths, placement):
    ctx_count = lax.axis_size("ctx")
    grp_count = lax.axis_size("grp")
    ctx_index = lax.axis_index("ctx")
    grp_index = lax.axis_index("grp")
    tile = (ROWS, HEAD)
    bf16 = functools.partial(jax.ShapeDtypeStruct, dtype=jnp.bfloat16)
    exchange = functools.partial(
        lax.all_to_all, axis_name="ctx", split_axis=0, concat_axis=0, tiled=True
    )

    doc_ends = jnp.cumsum(doc_lengths)
    doc_starts = doc_ends - doc_lengths
    blocks = lax.dynamic_slice_in_dim(placement, 2 * ctx_index, 2)
    start = (grp_index * SLOTS + blocks) * BLOCK
    q_pos = (start[:, None] + jnp.arange(BLOCK, dtype=jnp.int32)).reshape(-1)
    first = jnp.max(
        jnp.where(doc_starts[None, :] <= q_pos[:, None], doc_starts[None, :], 0), axis=1
    )
    low = first.reshape(2, BLOCK) - (start - LIMIT)[:, None]
    low = jnp.tile(low, (1, CHUNK)).reshape(2, 1, CHUNK * BLOCK)

    (packed,) = call(
        pack_kernel,
        [bf16((PIECES, 2, *tile))],
        [VMEM],
        jnp.stack([key_tensor, value_tensor]),
    )
    place = jnp.clip(placement, 0, SLOTS - 1)
    pieces = exchange(packed).reshape(SLOTS, *tile)
    ordered, last = call(
        order_kernel,
        [bf16((SLOTS, *tile)), bf16((BEFORE, *tile))],
        [SMEM, VMEM],
        place,
        pieces,
    )
    prev = lax.ppermute(last, "grp", [(i, i + 1) for i in range(grp_count - 1)])
    wanted, done = call(
        spread_kernel,
        [bf16((SLOTS, BEFORE, *tile)), jax.ShapeDtypeStruct((8, HEAD), jnp.float32)],
        [SMEM, VMEM, VMEM],
        place,
        ordered,
        prev,
        scratch=[pltpu.VMEM((SLOTS + BEFORE, *tile), jnp.bfloat16)],
    )
    far = exchange(wanted.reshape(ctx_count, 2, BEFORE, *tile))
    far = far.reshape(2, KV_HEADS, PARTS, 2, BEFORE, *tile)
    (stat,) = attend_own(low, queries, out_grad, key_tensor, value_tensor, done)
    far_grad, low = attend_far(low, queries, out_grad, stat, far)
    attended, query_grad, own_k, own_v = attend_rest(
        low, queries, out_grad, key_tensor, value_tensor, far
    )

    parts = exchange(far_grad.reshape(ctx_count, 2, BEFORE, *tile))
    parts = parts.reshape(SLOTS, BEFORE, *tile)
    slot_of = pltpu.SMEM((SLOTS,), jnp.int32)
    (ahead,) = call(
        head_kernel,
        [bf16((BEFORE, *tile))],
        [SMEM, VMEM, ANY],
        place,
        parts,
        own_k,
        scratch=[slot_of],
    )
    behind = lax.ppermute(ahead, "grp", [(i + 1, i) for i in range(grp_count - 1)])
    sums, tail = call(
        sum_kernel,
        [bf16((SLOTS, *tile)), jax.ShapeDtypeStruct((BEFORE, *tile), jnp.float32)],
        [SMEM, VMEM],
        place,
        parts,
        scratch=[slot_of],
    )
    (sums,) = call(
        tail_kernel,
        [bf16((SLOTS, *tile))],
        [SMEM, VMEM, VMEM, VMEM],
        place,
        sums,
        tail,
        behind,
        scratch=[slot_of],
    )
    sums = exchange(sums.reshape(ctx_count, 2, *tile))
    key_grad, value_grad = call(
        finish_kernel,
        [bf16(key_tensor.shape), bf16(value_tensor.shape)],
        [VMEM] * 3,
        sums,
        own_k,
        own_v,
    )
    return attended, query_grad, key_grad, value_grad


def solution(mesh):
    rows = P(("grp", "ctx"), None)
    return jax.shard_map(
        body,
        mesh=mesh,
        in_specs=(rows, rows, rows, rows, P(), P()),
        out_specs=(rows, rows, rows, rows),
        check_vma=False,
    )
```

```python
import functools
import math

import jax
import jax.numpy as jnp
from jax import lax
from jax.experimental import pallas as pl
from jax.experimental.pallas import tpu as pltpu
from jax.sharding import PartitionSpec as P

KV_HEADS = 4
GROUP_WIDTH = 16
HEAD = 128
LIMIT = 192
BLOCK = 64
SLOTS = 64
BEFORE = LIMIT // BLOCK
ROWS = 16
PARTS = BLOCK // ROWS
PIECES = 2 * KV_HEADS * PARTS
CHUNK = 4
SCALE = 1.0 / math.sqrt(HEAD)
LOG2E = math.log2(math.e)
MIB = 1024 * 1024

VMEM = pl.BlockSpec(memory_space=pltpu.VMEM)
SMEM = pl.BlockSpec(memory_space=pltpu.SMEM)
ANY = pl.BlockSpec(memory_space=pltpu.HBM)


def pack_kernel(rows_ref, out_ref):
    for tensor in range(2):
        for head in range(KV_HEADS):
            for part in range(PARTS):
                piece = (tensor * KV_HEADS + head) * PARTS + part
                for half in range(2):
                    out_ref[piece, half] = rows_ref[
                        tensor,
                        pl.ds(half * BLOCK + part * ROWS, ROWS),
                        pl.ds(head * HEAD, HEAD),
                    ]


def order_kernel(place_ref, pieces_ref, ordered_ref, last_ref):
    for slot in range(SLOTS):
        ordered_ref[place_ref[slot]] = pieces_ref[slot]
    last_ref[...] = ordered_ref[SLOTS - BEFORE :]


def spread_kernel(place_ref, ordered_ref, prev_ref, out_ref, done_ref, whole):
    whole[:BEFORE] = prev_ref[...]
    whole[BEFORE:] = ordered_ref[...]
    done_ref[...] = jnp.zeros_like(done_ref)
    for slot in range(SLOTS):
        out_ref[slot] = whole[pl.ds(place_ref[slot], BEFORE)]


def slots_of(place_ref, slot_of):
    for slot in range(SLOTS):
        slot_of[place_ref[slot]] = slot


def part_sum(slot_of, parts_ref, block):
    return sum(
        parts_ref[slot_of[block + ahead], BEFORE - ahead].astype(jnp.float32)
        for ahead in range(1, BEFORE + 1)
        if 0 <= block + ahead < SLOTS
    )


def head_kernel(place_ref, parts_ref, after_ref, out_ref, slot_of, early, sems):
    slots_of(place_ref, slot_of)
    copies = [
        pltpu.make_async_copy(parts_ref.at[slot_of[i]], early.at[i], sems.at[i])
        for i in range(BEFORE)
    ]
    for copy in copies:
        copy.start()
    for copy in copies:
        copy.wait()
    for back in range(BEFORE):
        total = sum(
            early[block, back - block].astype(jnp.float32) for block in range(back + 1)
        )
        out_ref[back] = total.astype(jnp.bfloat16)


def sum_kernel(place_ref, parts_ref, sums_ref, tail_ref, slot_of):
    slots_of(place_ref, slot_of)
    for block in range(SLOTS - 1):
        total = part_sum(slot_of, parts_ref, block)
        sums_ref[slot_of[block]] = total.astype(jnp.bfloat16)
        if block >= SLOTS - BEFORE:
            tail_ref[block - (SLOTS - BEFORE)] = total
    tail_ref[BEFORE - 1] = jnp.zeros((ROWS, HEAD), jnp.float32)


def tail_kernel(place_ref, sums_ref, tail_ref, next_ref, out_ref, slot_of):
    out_ref[...] = sums_ref[...]
    slots_of(place_ref, slot_of)
    for tail in range(BEFORE):
        total = tail_ref[tail] + next_ref[tail].astype(jnp.float32)
        out_ref[slot_of[SLOTS - BEFORE + tail]] = total.astype(jnp.bfloat16)


def finish_kernel(pieces_ref, dk_ref, dv_ref, out_k_ref, out_v_ref):
    for tensor, (own, out) in enumerate(((dk_ref, out_k_ref), (dv_ref, out_v_ref))):
        for head in range(KV_HEADS):
            for part in range(PARTS):
                piece = (tensor * KV_HEADS + head) * PARTS + part
                for half in range(2):
                    place = (
                        pl.ds(half * BLOCK + part * ROWS, ROWS),
                        pl.ds(head * HEAD, HEAD),
                    )
                    out[place] = (
                        own[place] + pieces_ref[piece, half].astype(jnp.float32)
                    ).astype(jnp.bfloat16)


def rows_of(ref, first, width=CHUNK):
    return jnp.concatenate(
        [ref[:, pl.ds((first + i) * HEAD, HEAD)] for i in range(width)], axis=0
    )


NT = (((1,), (1,)), ((), ()))
NN = (((1,), (0,)), ((), ()))
dot = functools.partial(lax.dot_general, preferred_element_type=jnp.float32)


def far_rows(far_ref, tensor, head, half):
    return [
        far_ref[tensor, head, part, half, back]
        for back in range(BEFORE)
        for part in range(PARTS)
    ]


def own_kernel(
    low_ref, q_ref, g_ref, k_ref, v_ref, after_ref, stat_ref, bias_ref
):
    key_index = LIMIT + lax.broadcasted_iota(jnp.int32, bias_ref.shape[1:], 0)
    query_index = lax.broadcasted_iota(jnp.int32, bias_ref.shape[1:], 1) % BLOCK
    for half in range(2):
        allowed = (key_index <= query_index + LIMIT) & (key_index >= low_ref[half])
        bias_ref[half] = jnp.where(allowed, 0.0, -1e30)

    for half in range(2):
        rows = pl.ds(half * BLOCK, BLOCK)
        for head in range(KV_HEADS):
            cols = pl.ds(head * HEAD, HEAD)
            for first in range(0, GROUP_WIDTH, CHUNK):
                lanes = pl.ds(first * BLOCK, CHUNK * BLOCK)
                query = rows_of(q_ref.at[rows], head * GROUP_WIDTH + first)
                grad = rows_of(g_ref.at[rows], head * GROUP_WIDTH + first)
                scores = dot(k_ref[rows, cols], query, NT) * (SCALE * LOG2E) + bias_ref[half]
                dprob = dot(v_ref[rows, cols], grad, NT)
                top = jnp.max(scores, axis=0, keepdims=True)
                raw = jnp.exp2(scores - top)
                stat_ref[half, head, 0:1, lanes] = top
                stat_ref[half, head, 1:2, lanes] = jnp.sum(raw, axis=0, keepdims=True)
                stat_ref[half, head, 2:3, lanes] = jnp.sum(raw * dprob, axis=0, keepdims=True)


def far_kernel(
    low_ref, q_ref, g_ref, stat_ref, far_ref, far_grad_ref, low_out_ref,
    bias_ref, q_rows, g_rows, sems,
):
    steps = [(half, head) for half in range(2) for head in range(KV_HEADS)]
    cuts = (0, 1, 4, 8)
    loads = {}
    for i, (first, last) in enumerate(zip(cuts[:-1], cuts[1:])):
        half, head = steps[first]
        place = (
            pl.ds(half * BLOCK, BLOCK),
            pl.ds(head * GROUP_WIDTH * HEAD, (last - first) * GROUP_WIDTH * HEAD),
        )
        loads[first] = [
            pltpu.make_async_copy(ref.at[place], rows.at[place], sems.at[i, j])
            for j, (ref, rows) in enumerate(((q_ref, q_rows), (g_ref, g_rows)))
        ]
        for load in loads[first]:
            load.start()
    low_out_ref[...] = low_ref[...]
    lanes = GROUP_WIDTH * BLOCK
    key_index = lax.broadcasted_iota(jnp.int32, (LIMIT, CHUNK * BLOCK), 0)
    for half in range(2):
        bias = jnp.where(key_index >= low_ref[half], 0.0, -1e30)
        bias_ref[half] = jnp.concatenate([bias] * (GROUP_WIDTH // CHUNK), axis=1)

    for step, (half, head) in enumerate(steps):
        rows = pl.ds(half * BLOCK, BLOCK)
        for load in loads.get(step, ()):
            load.wait()
        first = head * GROUP_WIDTH
        keys = jnp.concatenate(far_rows(far_ref, 0, head, half), axis=0)
        values = jnp.concatenate(far_rows(far_ref, 1, head, half), axis=0)
        query = rows_of(q_rows.at[rows], first, GROUP_WIDTH)
        grad = rows_of(g_rows.at[rows], first, GROUP_WIDTH)
        scores = dot(keys, query, NT) * (SCALE * LOG2E) + bias_ref[half]
        dprob = dot(values, grad, NT)
        own_top, own_total, own_delta = [
            stat_ref[half, head, i : i + 1, :lanes] for i in range(3)
        ]
        top = jnp.maximum(own_top, jnp.max(scores, axis=0, keepdims=True))
        raw = jnp.exp2(scores - top)
        fade = jnp.exp2(own_top - top)
        total = own_total * fade + jnp.sum(raw, axis=0, keepdims=True)
        delta = own_delta * fade + jnp.sum(raw * dprob, axis=0, keepdims=True)
        share = 1.0 / total
        weights = raw * share
        dscore = (weights * (dprob - delta * share)).astype(jnp.bfloat16)
        key_grad = dot(dscore, query, NN) * SCALE
        value_grad = dot(weights.astype(jnp.bfloat16), grad, NN)
        for tensor, grads in ((0, key_grad), (1, value_grad)):
            rounded = grads.astype(jnp.bfloat16)
            for back in range(BEFORE):
                for part in range(PARTS):
                    row = back * BLOCK + part * ROWS
                    far_grad_ref[tensor, head, part, half, back] = rounded[row : row + ROWS]


def rest_kernel(
    low_ref, q_ref, g_ref, k_ref, v_ref, far_ref, att_out_ref, dq_out_ref, dk_ref, dv_ref,
    bias_ref, q_rows, g_rows, att_rows, dq_rows, load_sems, store_sems,
):
    loads = [
        [
            pltpu.make_async_copy(
                ref.at[pl.ds(half * BLOCK, BLOCK)],
                rows.at[pl.ds(half * BLOCK, BLOCK)],
                load_sems.at[half, i],
            )
            for i, (ref, rows) in enumerate(((q_ref, q_rows), (g_ref, g_rows)))
        ]
        for half in range(2)
    ]
    for load in loads[0] + loads[1]:
        load.start()
    key_index = lax.broadcasted_iota(jnp.int32, (LIMIT + BLOCK, CHUNK * BLOCK), 0)
    query_index = lax.broadcasted_iota(jnp.int32, key_index.shape, 1) % BLOCK
    for half in range(2):
        allowed = (key_index <= query_index + LIMIT) & (key_index >= low_ref[half])
        bias = jnp.where(allowed, 0.0, -1e30)
        bias_ref[half] = jnp.concatenate([bias] * (GROUP_WIDTH // CHUNK), axis=1)

    def put(ref, cols):
        rows = cols.T.astype(jnp.bfloat16)
        for i in range(GROUP_WIDTH):
            ref[:, pl.ds(i * HEAD, HEAD)] = rows[i * BLOCK : (i + 1) * BLOCK]

    stores = []
    for half in range(2):
        rows = pl.ds(half * BLOCK, BLOCK)
        for load in loads[half]:
            load.wait()
        for head in range(KV_HEADS):
            cols = pl.ds(head * HEAD, HEAD)
            wide = pl.ds(head * GROUP_WIDTH * HEAD, GROUP_WIDTH * HEAD)
            keys = jnp.concatenate(far_rows(far_ref, 0, head, half) + [k_ref[rows, cols]], axis=0)
            values = jnp.concatenate(
                far_rows(far_ref, 1, head, half) + [v_ref[rows, cols]], axis=0
            )
            query = rows_of(q_rows.at[rows], head * GROUP_WIDTH, GROUP_WIDTH)
            grad = rows_of(g_rows.at[rows], head * GROUP_WIDTH, GROUP_WIDTH)
            scores = dot(keys, query, NT) * (SCALE * LOG2E) + bias_ref[half]
            dprob = dot(values, grad, NT)
            raw = jnp.exp2(scores - jnp.max(scores, axis=0, keepdims=True))
            weights = raw * (1.0 / jnp.sum(raw, axis=0, keepdims=True))
            weights_low = weights.astype(jnp.bfloat16)
            put(att_rows.at[rows, wide], dot(values.T, weights_low, NN))
            delta = jnp.sum(weights * dprob, axis=0, keepdims=True)
            dscore = (weights * (dprob - delta)).astype(jnp.bfloat16)
            put(dq_rows.at[rows, wide], dot(keys.T, dscore, NN) * SCALE)
            dk_ref[rows, cols] = dot(dscore[LIMIT:], query, NN) * SCALE
            dv_ref[rows, cols] = dot(weights_low[LIMIT:], grad, NN)
            for i, (held, out) in enumerate(((att_rows, att_out_ref), (dq_rows, dq_out_ref))):
                store = pltpu.make_async_copy(
                    held.at[rows, wide], out.at[rows, wide], store_sems.at[half, head, i]
                )
                store.start()
                stores.append(store)
    for store in stores:
        store.wait()


def attend_own(low, queries, out_grad, key_tensor, value_tensor, after):
    return call(
        own_kernel,
        [jax.ShapeDtypeStruct((2, KV_HEADS, 8, GROUP_WIDTH * BLOCK), jnp.float32)],
        [VMEM] * 5 + [ANY],
        low, queries, out_grad, key_tensor, value_tensor, after,
        scratch=[pltpu.VMEM((2, BLOCK, CHUNK * BLOCK), jnp.float32)],
        limit=24 * MIB,
    )


def attend_far(low, queries, out_grad, stat, far):
    return call(
        far_kernel,
        [
            jax.ShapeDtypeStruct(far.shape, jnp.bfloat16),
            jax.ShapeDtypeStruct(low.shape, jnp.int32),
        ],
        [VMEM, ANY, ANY, VMEM, VMEM],
        low, queries, out_grad, stat, far,
        scratch=[
            pltpu.VMEM((2, LIMIT, GROUP_WIDTH * BLOCK), jnp.float32),
            pltpu.VMEM(queries.shape, jnp.bfloat16),
            pltpu.VMEM(queries.shape, jnp.bfloat16),
            pltpu.SemaphoreType.DMA((3, 2)),
        ],
        limit=52 * MIB,
    )


def attend_rest(low, queries, out_grad, key_tensor, value_tensor, far):
    wide = jax.ShapeDtypeStruct(queries.shape, jnp.bfloat16)
    narrow = jax.ShapeDtypeStruct(key_tensor.shape, jnp.float32)
    return call(
        rest_kernel,
        [wide, wide, narrow, narrow],
        [VMEM, ANY, ANY, VMEM, VMEM, VMEM],
        low, queries, out_grad, key_tensor, value_tensor, far,
        out_specs=[ANY, ANY, VMEM, VMEM],
        scratch=[
            pltpu.VMEM((2, LIMIT + BLOCK, GROUP_WIDTH * BLOCK), jnp.float32),
            *[pltpu.VMEM(queries.shape, jnp.bfloat16)] * 4,
            pltpu.SemaphoreType.DMA((2, 2)),
            pltpu.SemaphoreType.DMA((2, KV_HEADS, 2)),
        ],
        limit=52 * MIB,
    )


def call(kernel, outs, specs, *args, out_specs=None, scratch=(), limit=8 * MIB):
    return pl.pallas_call(
        kernel,
        in_specs=specs,
        out_specs=out_specs or [VMEM] * len(outs),
        out_shape=outs,
        scratch_shapes=scratch,
        compiler_params=pltpu.CompilerParams(vmem_limit_bytes=limit),
    )(*args)


def body(queries, key_tensor, value_tensor, out_grad, doc_lengths, placement):
    ctx_count = lax.axis_size("ctx")
    grp_count = lax.axis_size("grp")
    ctx_index = lax.axis_index("ctx")
    grp_index = lax.axis_index("grp")
    tile = (ROWS, HEAD)
    bf16 = functools.partial(jax.ShapeDtypeStruct, dtype=jnp.bfloat16)
    exchange = functools.partial(
        lax.all_to_all, axis_name="ctx", split_axis=0, concat_axis=0, tiled=True
    )

    doc_ends = jnp.cumsum(doc_lengths)
    doc_starts = doc_ends - doc_lengths
    blocks = lax.dynamic_slice_in_dim(placement, 2 * ctx_index, 2)
    start = (grp_index * SLOTS + blocks) * BLOCK
    q_pos = (start[:, None] + jnp.arange(BLOCK, dtype=jnp.int32)).reshape(-1)
    first = jnp.max(
        jnp.where(doc_starts[None, :] <= q_pos[:, None], doc_starts[None, :], 0), axis=1
    )
    low = first.reshape(2, BLOCK) - (start - LIMIT)[:, None]
    low = jnp.tile(low, (1, CHUNK)).reshape(2, 1, CHUNK * BLOCK)

    (packed,) = call(
        pack_kernel,
        [bf16((PIECES, 2, *tile))],
        [VMEM],
        jnp.stack([key_tensor, value_tensor]),
    )
    place = jnp.clip(placement, 0, SLOTS - 1)
    pieces = exchange(packed).reshape(SLOTS, *tile)
    ordered, last = call(
        order_kernel,
        [bf16((SLOTS, *tile)), bf16((BEFORE, *tile))],
        [SMEM, VMEM],
        place,
        pieces,
    )
    prev = lax.ppermute(last, "grp", [(i, i + 1) for i in range(grp_count - 1)])
    wanted, done = call(
        spread_kernel,
        [bf16((SLOTS, BEFORE, *tile)), jax.ShapeDtypeStruct((8, HEAD), jnp.float32)],
        [SMEM, VMEM, VMEM],
        place,
        ordered,
        prev,
        scratch=[pltpu.VMEM((SLOTS + BEFORE, *tile), jnp.bfloat16)],
    )
    far = exchange(wanted.reshape(ctx_count, 2, BEFORE, *tile))
    far = far.reshape(2, KV_HEADS, PARTS, 2, BEFORE, *tile)
    (stat,) = attend_own(low, queries, out_grad, key_tensor, value_tensor, done)
    far_grad, low = attend_far(low, queries, out_grad, stat, far)
    attended, query_grad, own_k, own_v = attend_rest(
        low, queries, out_grad, key_tensor, value_tensor, far
    )

    parts = exchange(far_grad.reshape(ctx_count, 2, BEFORE, *tile))
    parts = parts.reshape(SLOTS, BEFORE, *tile)
    slot_of = pltpu.SMEM((SLOTS,), jnp.int32)
    (ahead,) = call(
        head_kernel,
        [bf16((BEFORE, *tile))],
        [SMEM, ANY, ANY],
        place,
        parts,
        own_k,
        scratch=[
            slot_of,
            pltpu.VMEM((BEFORE, BEFORE, *tile), jnp.bfloat16),
            pltpu.SemaphoreType.DMA((BEFORE,)),
        ],
    )
    behind = lax.ppermute(ahead, "grp", [(i + 1, i) for i in range(grp_count - 1)])
    sums, tail = call(
        sum_kernel,
        [bf16((SLOTS, *tile)), jax.ShapeDtypeStruct((BEFORE, *tile), jnp.float32)],
        [SMEM, VMEM],
        place,
        parts,
        scratch=[slot_of],
    )
    (sums,) = call(
        tail_kernel,
        [bf16((SLOTS, *tile))],
        [SMEM, VMEM, VMEM, VMEM],
        place,
        sums,
        tail,
        behind,
        scratch=[slot_of],
    )
    sums = exchange(sums.reshape(ctx_count, 2, *tile))
    key_grad, value_grad = call(
        finish_kernel,
        [bf16(key_tensor.shape), bf16(value_tensor.shape)],
        [VMEM] * 3,
        sums,
        own_k,
        own_v,
    )
    return attended, query_grad, key_grad, value_grad


def solution(mesh):
    rows = P(("grp", "ctx"), None)
    return jax.shard_map(
        body,
        mesh=mesh,
        in_specs=(rows, rows, rows, rows, P(), P()),
        out_specs=(rows, rows, rows, rows),
        check_vma=False,
    )
```

```python
import functools
import math

import jax
import jax.numpy as jnp
from jax import lax
from jax.experimental import pallas as pl
from jax.experimental.pallas import tpu as pltpu
from jax.sharding import PartitionSpec as P

KV_HEADS = 4
GROUP_WIDTH = 16
HEAD = 128
LIMIT = 192
BLOCK = 64
SLOTS = 64
BEFORE = LIMIT // BLOCK
ROWS = 16
PARTS = BLOCK // ROWS
PIECES = 2 * KV_HEADS * PARTS
CHUNK = 4
SCALE = 1.0 / math.sqrt(HEAD)
LOG2E = math.log2(math.e)
MIB = 1024 * 1024

VMEM = pl.BlockSpec(memory_space=pltpu.VMEM)
SMEM = pl.BlockSpec(memory_space=pltpu.SMEM)
ANY = pl.BlockSpec(memory_space=pltpu.HBM)


def pack_kernel(rows_ref, out_ref):
    for tensor in range(2):
        for head in range(KV_HEADS):
            for part in range(PARTS):
                piece = (tensor * KV_HEADS + head) * PARTS + part
                for half in range(2):
                    out_ref[piece, half] = rows_ref[
                        tensor,
                        pl.ds(half * BLOCK + part * ROWS, ROWS),
                        pl.ds(head * HEAD, HEAD),
                    ]


def order_kernel(place_ref, pieces_ref, ordered_ref, last_ref):
    for slot in range(SLOTS):
        ordered_ref[place_ref[slot]] = pieces_ref[slot]
    last_ref[...] = ordered_ref[SLOTS - BEFORE :]


def spread_kernel(
    late_ref, place_ref, ordered_ref, prev_ref, low_ref, q_ref, g_ref, kv_ref,
    out_ref, stat_ref, whole, *scratch,
):
    whole[:BEFORE] = prev_ref[...]
    whole[BEFORE:] = ordered_ref[...]
    for slot in range(SLOTS):
        out_ref[slot] = whole[pl.ds(place_ref[slot], BEFORE)]

    @pl.when(late_ref[0] != 0)
    def _():
        own_stats(low_ref, q_ref, g_ref, kv_ref, stat_ref, *scratch)


def slots_of(place_ref, slot_of):
    for slot in range(SLOTS):
        slot_of[place_ref[slot]] = slot


def part_sum(slot_of, parts_ref, block):
    return sum(
        parts_ref[slot_of[block + ahead], BEFORE - ahead].astype(jnp.float32)
        for ahead in range(1, BEFORE + 1)
        if 0 <= block + ahead < SLOTS
    )


def head_kernel(place_ref, parts_ref, after_ref, out_ref, slot_of, early, sems):
    slots_of(place_ref, slot_of)
    copies = [
        pltpu.make_async_copy(parts_ref.at[slot_of[i]], early.at[i], sems.at[i])
        for i in range(BEFORE)
    ]
    for copy in copies:
        copy.start()
    for copy in copies:
        copy.wait()
    for back in range(BEFORE):
        total = sum(
            early[block, back - block].astype(jnp.float32) for block in range(back + 1)
        )
        out_ref[back] = total.astype(jnp.bfloat16)


def sum_kernel(place_ref, parts_ref, sums_ref, tail_ref, slot_of):
    slots_of(place_ref, slot_of)
    for block in range(SLOTS - 1):
        total = part_sum(slot_of, parts_ref, block)
        sums_ref[slot_of[block]] = total.astype(jnp.bfloat16)
        if block >= SLOTS - BEFORE:
            tail_ref[block - (SLOTS - BEFORE)] = total
    tail_ref[BEFORE - 1] = jnp.zeros((ROWS, HEAD), jnp.float32)


def tail_kernel(place_ref, sums_ref, tail_ref, next_ref, out_ref, slot_of):
    out_ref[...] = sums_ref[...]
    slots_of(place_ref, slot_of)
    for tail in range(BEFORE):
        total = tail_ref[tail] + next_ref[tail].astype(jnp.float32)
        out_ref[slot_of[SLOTS - BEFORE + tail]] = total.astype(jnp.bfloat16)


def finish_kernel(pieces_ref, dk_ref, dv_ref, out_k_ref, out_v_ref):
    for tensor, (own, out) in enumerate(((dk_ref, out_k_ref), (dv_ref, out_v_ref))):
        for head in range(KV_HEADS):
            for part in range(PARTS):
                piece = (tensor * KV_HEADS + head) * PARTS + part
                for half in range(2):
                    place = (
                        pl.ds(half * BLOCK + part * ROWS, ROWS),
                        pl.ds(head * HEAD, HEAD),
                    )
                    out[place] = (
                        own[place] + pieces_ref[piece, half].astype(jnp.float32)
                    ).astype(jnp.bfloat16)


def rows_of(ref, first, width=CHUNK):
    return jnp.concatenate(
        [ref[:, pl.ds((first + i) * HEAD, HEAD)] for i in range(width)], axis=0
    )


NT = (((1,), (1,)), ((), ()))
NN = (((1,), (0,)), ((), ()))
dot = functools.partial(lax.dot_general, preferred_element_type=jnp.float32)


def far_rows(far_ref, tensor, head, half):
    return [
        far_ref[tensor, head, part, half, back]
        for back in range(BEFORE)
        for part in range(PARTS)
    ]


def own_stats(low_ref, q_ref, g_ref, kv_ref, stat_ref, bias_ref, rows_ref, sems):
    loads = [
        [
            pltpu.make_async_copy(
                ref.at[pl.ds(half * BLOCK, BLOCK)], rows_ref.at[half, i], sems.at[half, i]
            )
            for i, ref in enumerate((q_ref, g_ref))
        ]
        for half in range(2)
    ]
    for load in loads[0] + loads[1]:
        load.start()
    key_index = LIMIT + lax.broadcasted_iota(jnp.int32, bias_ref.shape[1:], 0)
    query_index = lax.broadcasted_iota(jnp.int32, bias_ref.shape[1:], 1) % BLOCK
    for half in range(2):
        allowed = (key_index <= query_index + LIMIT) & (key_index >= low_ref[half])
        bias_ref[half] = jnp.where(allowed, 0.0, -1e30)

    for half in range(2):
        rows = pl.ds(half * BLOCK, BLOCK)
        for load in loads[half]:
            load.wait()
        for head in range(KV_HEADS):
            cols = pl.ds(head * HEAD, HEAD)
            for first in range(0, GROUP_WIDTH, CHUNK):
                lanes = pl.ds(first * BLOCK, CHUNK * BLOCK)
                query = rows_of(rows_ref.at[half, 0], head * GROUP_WIDTH + first)
                grad = rows_of(rows_ref.at[half, 1], head * GROUP_WIDTH + first)
                scores = dot(kv_ref[0, rows, cols], query, NT) * (SCALE * LOG2E) + bias_ref[half]
                dprob = dot(kv_ref[1, rows, cols], grad, NT)
                top = jnp.max(scores, axis=0, keepdims=True)
                raw = jnp.exp2(scores - top)
                stat_ref[half, head, 0:1, lanes] = top
                stat_ref[half, head, 1:2, lanes] = jnp.sum(raw, axis=0, keepdims=True)
                stat_ref[half, head, 2:3, lanes] = jnp.sum(raw * dprob, axis=0, keepdims=True)


OWN_SCRATCH = [
    pltpu.VMEM((2, BLOCK, CHUNK * BLOCK), jnp.float32),
    pltpu.VMEM((2, 2, BLOCK, KV_HEADS * GROUP_WIDTH * HEAD), jnp.bfloat16),
    pltpu.SemaphoreType.DMA((2, 2)),
]
STAT = jax.ShapeDtypeStruct((2, KV_HEADS, 8, GROUP_WIDTH * BLOCK), jnp.float32)


def own_kernel(
    late_ref, before_ref, low_ref, q_ref, g_ref, kv_ref, stat_ref, *scratch
):
    late = late_ref[0]

    @pl.when(late == 0)
    def _():
        own_stats(low_ref, q_ref, g_ref, kv_ref, stat_ref, *scratch)

    @pl.when(late != 0)
    def _():
        stat_ref[...] = before_ref[...]


def far_kernel(
    low_ref, q_ref, g_ref, stat_ref, far_ref, far_grad_ref, low_out_ref,
    bias_ref, q_rows, g_rows, sems,
):
    steps = [(half, head) for half in range(2) for head in range(KV_HEADS)]
    cuts = (0, 1, 4, 8)
    loads = {}
    for i, (first, last) in enumerate(zip(cuts[:-1], cuts[1:])):
        half, head = steps[first]
        place = (
            pl.ds(half * BLOCK, BLOCK),
            pl.ds(head * GROUP_WIDTH * HEAD, (last - first) * GROUP_WIDTH * HEAD),
        )
        loads[first] = [
            pltpu.make_async_copy(ref.at[place], rows.at[place], sems.at[i, j])
            for j, (ref, rows) in enumerate(((q_ref, q_rows), (g_ref, g_rows)))
        ]
        for load in loads[first]:
            load.start()
    low_out_ref[...] = low_ref[...]
    lanes = GROUP_WIDTH * BLOCK
    key_index = lax.broadcasted_iota(jnp.int32, (LIMIT, CHUNK * BLOCK), 0)
    for half in range(2):
        bias = jnp.where(key_index >= low_ref[half], 0.0, -1e30)
        bias_ref[half] = jnp.concatenate([bias] * (GROUP_WIDTH // CHUNK), axis=1)

    for step, (half, head) in enumerate(steps):
        rows = pl.ds(half * BLOCK, BLOCK)
        for load in loads.get(step, ()):
            load.wait()
        first = head * GROUP_WIDTH
        keys = jnp.concatenate(far_rows(far_ref, 0, head, half), axis=0)
        values = jnp.concatenate(far_rows(far_ref, 1, head, half), axis=0)
        query = rows_of(q_rows.at[rows], first, GROUP_WIDTH)
        grad = rows_of(g_rows.at[rows], first, GROUP_WIDTH)
        scores = dot(keys, query, NT) * (SCALE * LOG2E) + bias_ref[half]
        dprob = dot(values, grad, NT)
        own_top, own_total, own_delta = [
            stat_ref[half, head, i : i + 1, :lanes] for i in range(3)
        ]
        top = jnp.maximum(own_top, jnp.max(scores, axis=0, keepdims=True))
        raw = jnp.exp2(scores - top)
        fade = jnp.exp2(own_top - top)
        total = own_total * fade + jnp.sum(raw, axis=0, keepdims=True)
        delta = own_delta * fade + jnp.sum(raw * dprob, axis=0, keepdims=True)
        share = 1.0 / total
        weights = raw * share
        dscore = (weights * (dprob - delta * share)).astype(jnp.bfloat16)
        key_grad = dot(dscore, query, NN) * SCALE
        value_grad = dot(weights.astype(jnp.bfloat16), grad, NN)
        for tensor, grads in ((0, key_grad), (1, value_grad)):
            rounded = grads.astype(jnp.bfloat16)
            for back in range(BEFORE):
                for part in range(PARTS):
                    row = back * BLOCK + part * ROWS
                    far_grad_ref[tensor, head, part, half, back] = rounded[row : row + ROWS]


def rest_kernel(
    low_ref, q_ref, g_ref, k_ref, v_ref, far_ref, att_out_ref, dq_out_ref, dk_ref, dv_ref,
    bias_ref, q_rows, g_rows, att_rows, dq_rows, load_sems, store_sems,
):
    loads = [
        [
            pltpu.make_async_copy(
                ref.at[pl.ds(half * BLOCK, BLOCK)],
                rows.at[pl.ds(half * BLOCK, BLOCK)],
                load_sems.at[half, i],
            )
            for i, (ref, rows) in enumerate(((q_ref, q_rows), (g_ref, g_rows)))
        ]
        for half in range(2)
    ]
    for load in loads[0] + loads[1]:
        load.start()
    key_index = lax.broadcasted_iota(jnp.int32, (LIMIT + BLOCK, CHUNK * BLOCK), 0)
    query_index = lax.broadcasted_iota(jnp.int32, key_index.shape, 1) % BLOCK
    for half in range(2):
        allowed = (key_index <= query_index + LIMIT) & (key_index >= low_ref[half])
        bias = jnp.where(allowed, 0.0, -1e30)
        bias_ref[half] = jnp.concatenate([bias] * (GROUP_WIDTH // CHUNK), axis=1)

    def put(ref, cols):
        rows = cols.T.astype(jnp.bfloat16)
        for i in range(GROUP_WIDTH):
            ref[:, pl.ds(i * HEAD, HEAD)] = rows[i * BLOCK : (i + 1) * BLOCK]

    stores = []
    for half in range(2):
        rows = pl.ds(half * BLOCK, BLOCK)
        for load in loads[half]:
            load.wait()
        for head in range(KV_HEADS):
            cols = pl.ds(head * HEAD, HEAD)
            wide = pl.ds(head * GROUP_WIDTH * HEAD, GROUP_WIDTH * HEAD)
            keys = jnp.concatenate(far_rows(far_ref, 0, head, half) + [k_ref[rows, cols]], axis=0)
            values = jnp.concatenate(
                far_rows(far_ref, 1, head, half) + [v_ref[rows, cols]], axis=0
            )
            query = rows_of(q_rows.at[rows], head * GROUP_WIDTH, GROUP_WIDTH)
            grad = rows_of(g_rows.at[rows], head * GROUP_WIDTH, GROUP_WIDTH)
            scores = dot(keys, query, NT) * (SCALE * LOG2E) + bias_ref[half]
            dprob = dot(values, grad, NT)
            raw = jnp.exp2(scores - jnp.max(scores, axis=0, keepdims=True))
            weights = raw * (1.0 / jnp.sum(raw, axis=0, keepdims=True))
            weights_low = weights.astype(jnp.bfloat16)
            put(att_rows.at[rows, wide], dot(values.T, weights_low, NN))
            delta = jnp.sum(weights * dprob, axis=0, keepdims=True)
            dscore = (weights * (dprob - delta)).astype(jnp.bfloat16)
            put(dq_rows.at[rows, wide], dot(keys.T, dscore, NN) * SCALE)
            dk_ref[rows, cols] = dot(dscore[LIMIT:], query, NN) * SCALE
            dv_ref[rows, cols] = dot(weights_low[LIMIT:], grad, NN)
            for i, (held, out) in enumerate(((att_rows, att_out_ref), (dq_rows, dq_out_ref))):
                store = pltpu.make_async_copy(
                    held.at[rows, wide], out.at[rows, wide], store_sems.at[half, head, i]
                )
                store.start()
                stores.append(store)
    for store in stores:
        store.wait()


def attend_own(late, before, low, queries, out_grad, pair):
    return call(
        own_kernel,
        [STAT],
        [SMEM, VMEM, VMEM, ANY, ANY, VMEM],
        late, before, low, queries, out_grad, pair,
        scratch=OWN_SCRATCH,
        limit=52 * MIB,
    )


def attend_far(low, queries, out_grad, stat, far):
    return call(
        far_kernel,
        [
            jax.ShapeDtypeStruct(far.shape, jnp.bfloat16),
            jax.ShapeDtypeStruct(low.shape, jnp.int32),
        ],
        [VMEM, ANY, ANY, VMEM, VMEM],
        low, queries, out_grad, stat, far,
        scratch=[
            pltpu.VMEM((2, LIMIT, GROUP_WIDTH * BLOCK), jnp.float32),
            pltpu.VMEM(queries.shape, jnp.bfloat16),
            pltpu.VMEM(queries.shape, jnp.bfloat16),
            pltpu.SemaphoreType.DMA((3, 2)),
        ],
        limit=52 * MIB,
    )


def attend_rest(low, queries, out_grad, key_tensor, value_tensor, far):
    wide = jax.ShapeDtypeStruct(queries.shape, jnp.bfloat16)
    narrow = jax.ShapeDtypeStruct(key_tensor.shape, jnp.float32)
    return call(
        rest_kernel,
        [wide, wide, narrow, narrow],
        [VMEM, ANY, ANY, VMEM, VMEM, VMEM],
        low, queries, out_grad, key_tensor, value_tensor, far,
        out_specs=[ANY, ANY, VMEM, VMEM],
        scratch=[
            pltpu.VMEM((2, LIMIT + BLOCK, GROUP_WIDTH * BLOCK), jnp.float32),
            *[pltpu.VMEM(queries.shape, jnp.bfloat16)] * 4,
            pltpu.SemaphoreType.DMA((2, 2)),
            pltpu.SemaphoreType.DMA((2, KV_HEADS, 2)),
        ],
        limit=52 * MIB,
    )


def call(kernel, outs, specs, *args, out_specs=None, scratch=(), limit=8 * MIB):
    return pl.pallas_call(
        kernel,
        in_specs=specs,
        out_specs=out_specs or [VMEM] * len(outs),
        out_shape=outs,
        scratch_shapes=scratch,
        compiler_params=pltpu.CompilerParams(vmem_limit_bytes=limit),
    )(*args)


def body(queries, key_tensor, value_tensor, out_grad, doc_lengths, placement):
    ctx_count = lax.axis_size("ctx")
    grp_count = lax.axis_size("grp")
    ctx_index = lax.axis_index("ctx")
    grp_index = lax.axis_index("grp")
    tile = (ROWS, HEAD)
    bf16 = functools.partial(jax.ShapeDtypeStruct, dtype=jnp.bfloat16)
    exchange = functools.partial(
        lax.all_to_all, axis_name="ctx", split_axis=0, concat_axis=0, tiled=True
    )

    doc_ends = jnp.cumsum(doc_lengths)
    doc_starts = doc_ends - doc_lengths
    blocks = lax.dynamic_slice_in_dim(placement, 2 * ctx_index, 2)
    start = (grp_index * SLOTS + blocks) * BLOCK
    q_pos = (start[:, None] + jnp.arange(BLOCK, dtype=jnp.int32)).reshape(-1)
    first = jnp.max(
        jnp.where(doc_starts[None, :] <= q_pos[:, None], doc_starts[None, :], 0), axis=1
    )
    low = first.reshape(2, BLOCK) - (start - LIMIT)[:, None]
    low = jnp.tile(low, (1, CHUNK)).reshape(2, 1, CHUNK * BLOCK)

    late = ((grp_index == 1) | ((grp_index % 2 == 0) & (grp_index > 0))).astype(jnp.int32)
    late = late.reshape(1)

    pair = jnp.stack([key_tensor, value_tensor])
    (packed,) = call(
        pack_kernel,
        [bf16((PIECES, 2, *tile))],
        [VMEM],
        pair,
    )
    place = jnp.clip(placement, 0, SLOTS - 1)
    pieces = exchange(packed).reshape(SLOTS, *tile)
    ordered, last = call(
        order_kernel,
        [bf16((SLOTS, *tile)), bf16((BEFORE, *tile))],
        [SMEM, VMEM],
        place,
        pieces,
    )
    prev = lax.ppermute(last, "grp", [(i, i + 1) for i in range(grp_count - 1)])
    wanted, before = call(
        spread_kernel,
        [bf16((SLOTS, BEFORE, *tile)), STAT],
        [SMEM, SMEM, VMEM, VMEM, VMEM, ANY, ANY, VMEM],
        late, place, ordered, prev, low, queries, out_grad, pair,
        scratch=[pltpu.VMEM((SLOTS + BEFORE, *tile), jnp.bfloat16), *OWN_SCRATCH],
        limit=52 * MIB,
    )
    far = exchange(wanted.reshape(ctx_count, 2, BEFORE, *tile))
    far = far.reshape(2, KV_HEADS, PARTS, 2, BEFORE, *tile)
    (stat,) = attend_own(late, before, low, queries, out_grad, pair)
    far_grad, low = attend_far(low, queries, out_grad, stat, far)
    attended, query_grad, own_k, own_v = attend_rest(
        low, queries, out_grad, key_tensor, value_tensor, far
    )

    parts = exchange(far_grad.reshape(ctx_count, 2, BEFORE, *tile))
    parts = parts.reshape(SLOTS, BEFORE, *tile)
    slot_of = pltpu.SMEM((SLOTS,), jnp.int32)
    (ahead,) = call(
        head_kernel,
        [bf16((BEFORE, *tile))],
        [SMEM, ANY, ANY],
        place,
        parts,
        own_k,
        scratch=[
            slot_of,
            pltpu.VMEM((BEFORE, BEFORE, *tile), jnp.bfloat16),
            pltpu.SemaphoreType.DMA((BEFORE,)),
        ],
    )
    behind = lax.ppermute(ahead, "grp", [(i + 1, i) for i in range(grp_count - 1)])
    sums, tail = call(
        sum_kernel,
        [bf16((SLOTS, *tile)), jax.ShapeDtypeStruct((BEFORE, *tile), jnp.float32)],
        [SMEM, VMEM],
        place,
        parts,
        scratch=[slot_of],
    )
    (sums,) = call(
        tail_kernel,
        [bf16((SLOTS, *tile))],
        [SMEM, VMEM, VMEM, VMEM],
        place,
        sums,
        tail,
        behind,
        scratch=[slot_of],
    )
    sums = exchange(sums.reshape(ctx_count, 2, *tile))
    key_grad, value_grad = call(
        finish_kernel,
        [bf16(key_tensor.shape), bf16(value_tensor.shape)],
        [VMEM] * 3,
        sums,
        own_k,
        own_v,
    )
    return attended, query_grad, key_grad, value_grad


def solution(mesh):
    rows = P(("grp", "ctx"), None)
    return jax.shard_map(
        body,
        mesh=mesh,
        in_specs=(rows, rows, rows, rows, P(), P()),
        out_specs=(rows, rows, rows, rows),
        check_vma=False,
    )
```
